32 devices in a mesh: qrow: 4 (over y, x), kcol: 4 (over z), dp: 2 (over core).
Axes of the slice: x: 2, y: 2, z: 4, core: 2. Of those that a mesh axis runs over, the one named last changes fastest.
Arguments:
- request_vectors: bfloat16 [192, 2048], P(('qrow', 'kcol'), 'dp'), may hold values from -6 to 6
- sequence_probes: bfloat16 [2048, 2048], P(('kcol', 'qrow'), 'dp'), may hold values from -6 to 6
- sequence_contents: bfloat16 [2048, 2048], P(('kcol', 'qrow'), 'dp'), may hold values from -6 to 6
- mixed_result: bfloat16 [192, 2048], P(('qrow', 'kcol'), 'dp'), may hold values from -4 to 4
- result_cotangent: bfloat16 [192, 2048], P(('qrow', 'kcol'), 'dp'), may hold values from -4 to 4
- saved_normalizer: float32 [16, 192], P('dp', ('qrow', 'kcol'))
- score_multiplier: float32 [16], P('dp'), may hold values from 0.5 to 2
- segment_spans: int32 [8], replicated, may hold values from 1 to 96, 192 in all
Outputs:
- grad_queries: bfloat16 [192, 2048], P(('qrow', 'kcol'), 'dp')
- grad_keys: bfloat16 [2048, 2048], P(('kcol', 'qrow'), 'dp')
- grad_values: bfloat16 [2048, 2048], P(('kcol', 'qrow'), 'dp')
- grad_temperature: float32 [16], replicated
The draws below stay inside these ranges and needn't reach their ends.
Inputs may be any that keep to these rules, and one draw needn't show every extreme that they name: `segment_spans`: 8 positive document lengths summing to 192; the longest is exactly 96.
All inputs are finite; a program needn't handle non-finite values.
Results may differ from the reference program's by a relative error of at most 0.01.
Values may be sent and summed in bfloat16 or wider, within the bound.
A program may use at most 64 MiB of HBM per device.

```python
import math
import jax
import jax.numpy as jnp
import numpy as np
from jax import lax

SHARD_CHANNELS = 16
HEAD_DIM = 128
DOCS = 8
SEQUENCE_LENGTH = 2048
RECENT_POSITIONS = 192
QBLOCK = 48
KBLOCK = 512
HD = 2048
N_QROW = 4
N_KCOL = 4


def draw_saved_normalizer(key, part):
    key = jax.random.fold_in(key, 7)
    positions = jnp.arange(RECENT_POSITIONS, dtype=jnp.float32) + (SEQUENCE_LENGTH - RECENT_POSITIONS)
    noise = jax.random.uniform(key, (SHARD_CHANNELS, RECENT_POSITIONS), jnp.float32, 0.5, 1.5)
    return jnp.log1p(positions)[None, :] + noise


def level_of(rng, dims, cuts, smallest, largest):
    def one(axis_at, blocks):
        draws = jax.random.uniform(jax.random.fold_in(jax.random.fold_in(rng, 6), axis_at), (blocks,), jnp.float32, smallest / len(cuts), largest / len(cuts))
        return jnp.repeat(jnp.exp(draws), dims[axis_at] // blocks).reshape((-1,) + (1,) * (len(dims) - axis_at - 1))

    level = one(*cuts[0])
    for cut in cuts[1:]:
        level = level * one(*cut)
    return level


def profile(number_of, total, bound, slope):
    portions = [(1 << 20) // math.isqrt(standing ** slope) + 1 for standing in range(2, number_of + 1)]
    spare, counts = total - bound - (number_of - 1), [1] * (number_of - 1)
    while spare > 0:
        free = [i for i in range(number_of - 1) if counts[i] < bound]
        pool, left = sum([portions[i] for i in free]), spare
        for i in free:
            extra = min(bound - counts[i], max(1, left * portions[i] // pool), spare)
            counts[i] = counts[i] + extra
            spare = spare - extra
    return np.array([bound] + counts)


def ragged_sizes(rng, amount, total, limit, skew):
    if amount == 2:
        one = jax.random.randint(rng, (), max(1, total - limit), min(limit, total - 1) + 1)
        return jnp.stack([one, total - one])
    lengths = jnp.asarray(profile(amount, total, limit, skew), jnp.int32)
    twos = (amount - 1) // 2
    source_of, sink = lengths[1:1 + 2 * twos:2], lengths[2:2 + 2 * twos:2]
    margin = jnp.minimum(source_of - 1, limit - sink)
    shifted = jax.random.randint(jax.random.fold_in(rng, 1), (twos,), 0, 1 << 20) % (margin + 1)
    lengths = lengths.at[1:1 + 2 * twos:2].set(source_of - shifted).at[2:2 + 2 * twos:2].set(sink + shifted)
    return lengths[jax.random.permutation(jax.random.fold_in(rng, 2), amount)]


def normal_values(own_key, shape, spread, bound, pieces=(), held_as=jnp.bfloat16):
    entries = jax.random.normal(own_key, shape, jnp.float32) * spread
    if len(pieces) > 0:
        entries = level_of(own_key, shape, pieces, -0.22, 0.18) * entries
    return jnp.clip(entries, min=-bound, max=bound).astype(held_as)


def setup_inputs(seed: int = 0) -> dict:
    keys = jax.random.split(jax.random.key(seed), 9)
    return {
        "request_vectors": normal_values(keys[0], (RECENT_POSITIONS, HD), 1.0, 6.0, ((0, 16), (1, 2))),
        "sequence_probes": normal_values(keys[1], (SEQUENCE_LENGTH, HD), 1.0, 6.0, ((0, 16), (1, 2))),
        "sequence_contents": normal_values(keys[2], (SEQUENCE_LENGTH, HD), 1.0, 6.0, ((0, 16), (1, 2))),
        "mixed_result": normal_values(keys[3], (RECENT_POSITIONS, HD), 0.25, 4.0, ((0, 16), (1, 2))),
        "result_cotangent": normal_values(keys[4], (RECENT_POSITIONS, HD), 0.25, 4.0, ((0, 16), (1, 2))),
        "saved_normalizer": draw_saved_normalizer(jax.random.fold_in(keys[8], 71), 0),
        "score_multiplier": jnp.clip(jnp.exp(math.log(2.0) - 1.3862944 * jax.random.uniform(keys[6], (SHARD_CHANNELS,), jnp.float32) ** level_of(keys[6], (SHARD_CHANNELS,), ((0, 2),), -0.2, 0.2)), 0.5, 2.0),
        "segment_spans": ragged_sizes(keys[7], DOCS, RECENT_POSITIONS, RECENT_POSITIONS // 2, 2).astype(jnp.int32),
    }


def reference(request_vectors, sequence_probes, sequence_contents, mixed_result, result_cotangent, saved_normalizer, score_multiplier, segment_spans):
    depth = HEAD_DIM
    factor_applied = 1.0 / math.sqrt(depth)
    offset = SEQUENCE_LENGTH - RECENT_POSITIONS
    q_pos = jnp.arange(RECENT_POSITIONS, dtype=jnp.int32) + offset
    k_pos = jnp.arange(SEQUENCE_LENGTH, dtype=jnp.int32)
    starts = (jnp.cumsum(segment_spans) - segment_spans).astype(jnp.int32) + offset
    q_start = lax.optimization_barrier(jnp.max(jnp.where(starts[None, :] <= q_pos[:, None], starts[None, :], offset), axis=1))
    allowed_mask = (k_pos[None, :] <= q_pos[:, None]) & ((k_pos[None, :] >= q_start[:, None]) | (k_pos[None, :] < offset))

    def divide_pieces(array, rows):
        return array.reshape(rows, SHARD_CHANNELS, depth).transpose(1, 0, 2)
    result_inner_product = (result_cotangent.astype(jnp.float32) * mixed_result.astype(jnp.float32)).reshape(RECENT_POSITIONS, SHARD_CHANNELS, depth).sum(axis=2).T

    def one_channel(entries_list):
        channel_requests, channel_probes, channel_contents, channel_cotangent, channel_normalizer, channel_correction, channel_multiplier = entries_list
        unscaled_logits = jnp.dot(channel_requests, channel_probes.T, preferred_element_type=jnp.float32) * factor_applied
        softmax_weight = jnp.where(allowed_mask, jnp.exp(channel_multiplier * unscaled_logits - channel_normalizer[:, None]), 0.0)
        prob_b = softmax_weight.astype(jnp.bfloat16)
        dprob = jnp.dot(channel_cotangent, channel_contents.T, preferred_element_type=jnp.float32)
        logit_cotangent = softmax_weight * (dprob - channel_correction[:, None])
        multiplier_cotangent = jnp.sum(logit_cotangent * unscaled_logits)
        probe_cotangent = (channel_multiplier * factor_applied * logit_cotangent).astype(jnp.bfloat16)
        terms_q = jnp.einsum('qjk,jkd->jqd', probe_cotangent.reshape(RECENT_POSITIONS, N_KCOL, KBLOCK).astype(jnp.float32), channel_probes.reshape(N_KCOL, KBLOCK, depth).astype(jnp.float32)).astype(jnp.bfloat16)
        terms_k = jnp.einsum('iqk,iqd->ikd', probe_cotangent.reshape(N_QROW, QBLOCK, SEQUENCE_LENGTH).astype(jnp.float32), channel_requests.reshape(N_QROW, QBLOCK, depth).astype(jnp.float32)).astype(jnp.bfloat16)
        terms_v = jnp.einsum('iqk,iqd->ikd', prob_b.reshape(N_QROW, QBLOCK, SEQUENCE_LENGTH).astype(jnp.float32), channel_cotangent.reshape(N_QROW, QBLOCK, depth).astype(jnp.float32)).astype(jnp.bfloat16)
        return (lax.optimization_barrier(jnp.sum(terms_q.astype(jnp.float32), axis=0)), lax.optimization_barrier(jnp.sum(terms_k.astype(jnp.float32), axis=0)), lax.optimization_barrier(jnp.sum(terms_v.astype(jnp.float32), axis=0)), multiplier_cotangent)
    request_sensitivity, probe_sensitivity, content_sensitivity, multiplier_sensitivity = lax.map(one_channel, (divide_pieces(request_vectors, RECENT_POSITIONS), divide_pieces(sequence_probes, SEQUENCE_LENGTH), divide_pieces(sequence_contents, SEQUENCE_LENGTH), divide_pieces(result_cotangent, RECENT_POSITIONS), saved_normalizer, result_inner_product, score_multiplier))

    def combine_channels(array, rows):
        return array.transpose(1, 0, 2).reshape(rows, SHARD_CHANNELS * depth).astype(jnp.bfloat16)
    return (combine_channels(request_sensitivity, RECENT_POSITIONS), combine_channels(probe_sensitivity, SEQUENCE_LENGTH), combine_channels(content_sensitivity, SEQUENCE_LENGTH), multiplier_sensitivity)
```

```python
import functools
import math

import jax
import jax.numpy as jnp
from jax import lax
from jax.experimental import pallas as pl
from jax.experimental.pallas import tpu as pltpu
from jax.sharding import PartitionSpec as P

MESH = pl.DeviceIdType.MESH
F32 = jnp.float32
BF16 = jnp.bfloat16


def kernel(
    dims,
    q_ref, k_ref, v_ref, o_ref, g_ref, lse_ref, mult_ref, spans_ref,
    dq_ref, dk_ref, dv_ref, tau_ref,
    pack32, asm32, gath, stat1, blk, stat, prob_s, grad_s, dqs, dqr, dq0, dqz, tau_acc, tau_a, tau_b,
    s1, r1, s1s, r1s, s2, r2, s2s, r2s, sa, ra, sb, rb, sta, rta, stb, rtb,
):
    n_rows, n_cols, n_dp, heads, depth, qs, ks, lanes = dims
    rows = n_cols * qs
    hq = heads * qs
    qrow = lax.axis_index("qrow")
    kcol = lax.axis_index("kcol")
    dp = lax.axis_index("dp")
    flat = dp * n_rows + qrow
    n_flat = n_dp * n_rows
    offset = (ks - qs) * n_rows * n_cols
    factor = 1.0 / math.sqrt(depth)

    barrier = pltpu.get_barrier_semaphore()

    @pl.loop(1, n_cols)
    def _(j):
        pl.semaphore_signal(
            barrier, inc=1, device_id={"kcol": lax.rem(kcol + j, n_cols)}, device_id_type=MESH
        )

    @pl.loop(1, n_flat)
    def _(t):
        peer = lax.rem(flat + t, n_flat)
        pl.semaphore_signal(
            barrier,
            inc=1,
            device_id={"qrow": lax.rem(peer, n_rows), "dp": peer // n_rows},
            device_id_type=MESH,
        )

    q32 = q_ref[...].astype(F32)
    g32 = g_ref[...].astype(F32)
    prod = g32 * o_ref[...].astype(F32)
    lane = lax.broadcasted_iota(jnp.int32, (qs, 128), 1)
    delta = jnp.zeros((qs, 128), F32)
    for h in range(heads):
        cols = slice(h * depth, (h + 1) * depth)
        pack32[h * qs : (h + 1) * qs, :] = q32[:, cols]
        pack32[hq + h * qs : hq + (h + 1) * qs, :] = g32[:, cols]
        delta = jnp.where(lane == h, jnp.sum(prod[:, cols], axis=1, keepdims=True), delta)
    gath[kcol] = pack32[...].astype(BF16)
    asm32[0:128, :] = jnp.zeros((128, 128), F32)
    asm32[0:qs, :] = delta
    delta_t = asm32[0:128, :].T
    asm32[0:heads, :] = jnp.zeros((heads, 128), F32)
    asm32[0:heads, 0:qs] = lse_ref[...]
    both = jnp.concatenate([asm32[0:heads, :], delta_t[0:heads, :]], axis=0)
    if lanes > 128:
        both = jnp.concatenate([both, jnp.zeros((2 * heads, lanes - 128), F32)], axis=1)
    stat1[kcol] = pltpu.roll(both, kcol * qs, 1)
    tau_acc[...] = jnp.zeros_like(tau_acc)

    pl.semaphore_wait(barrier, n_cols - 1 + n_flat - 1)

    def gather_copy(j, which):
        peer = {"kcol": lax.rem(kcol + j, n_cols)}
        buf, ss, rs = which
        return pltpu.make_async_remote_copy(
            src_ref=buf.at[kcol], dst_ref=buf.at[kcol],
            send_sem=ss.at[j], recv_sem=rs.at[j], device_id=peer, device_id_type=MESH,
        )

    first = ((gath, s1, r1), (stat1, s1s, r1s))

    @pl.loop(1, n_cols)
    def _(j):
        for which in first:
            gather_copy(j, which).start()

    def gather_wait(j):
        source = lax.rem(kcol - j + n_cols, n_cols)
        for buf, ss, rs in first:
            pltpu.make_async_remote_copy(
                src_ref=buf.at[source], dst_ref=buf.at[source],
                send_sem=ss.at[j], recv_sem=rs.at[j],
                device_id={"kcol": lax.rem(kcol + j, n_cols)}, device_id_type=MESH,
            ).wait_recv()

    @pl.loop(1, n_cols)
    def _(j):
        gather_wait(j)

    total = stat1[0]
    for z in range(1, n_cols):
        total = total + stat1[z]
    stat[0] = total
    for z in range(n_cols):
        pack32[...] = gath[z].astype(F32)
        for h in range(2 * heads):
            asm32[h * rows + z * qs : h * rows + (z + 1) * qs, :] = pack32[h * qs : (h + 1) * qs, :]
    blk[0] = asm32[...].astype(BF16)

    second = ((blk, s2, r2), (stat, s2s, r2s))

    def exchange_copy(i, which):
        buf, ss, rs = which
        return pltpu.make_async_remote_copy(
            src_ref=buf.at[0], dst_ref=buf.at[i],
            send_sem=ss.at[i], recv_sem=rs.at[i],
            device_id={"qrow": lax.rem(qrow + i, n_rows)}, device_id_type=MESH,
        )

    def term_copy(i):
        return pltpu.make_async_remote_copy(
            src_ref=dqs.at[i], dst_ref=dqr.at[i],
            send_sem=sa.at[i], recv_sem=ra.at[i],
            device_id={"qrow": lax.rem(qrow - i + n_rows, n_rows)}, device_id_type=MESH,
        )

    @pl.loop(1, n_rows)
    def _(i):
        for which in second:
            exchange_copy(i, which).start()

    k_pos = (kcol * n_rows + qrow) * ks + lax.broadcasted_iota(jnp.int32, (rows, ks), 1)

    def tile(i, own):
        group = lax.rem(qrow - i + n_rows, n_rows)
        columns = jnp.concatenate(
            [stat[i], jnp.zeros((128 - 2 * heads, lanes), F32)], axis=0
        ).T
        q_pos = offset + rows * group + lax.broadcasted_iota(jnp.int32, (rows, ks), 0)
        start = jnp.full((rows, ks), offset, jnp.int32)
        begin = offset
        for d in range(spans_ref.shape[0]):
            start = jnp.where(begin <= q_pos, begin, start)
            begin = begin + spans_ref[d]
        mask = (k_pos <= q_pos) & ((k_pos >= start) | (k_pos < offset))
        at = pl.ds(pl.multiple_of(i * rows, 16), rows)
        for h in range(heads):
            cols = slice(h * depth, (h + 1) * depth)
            q = blk[i, h * rows : (h + 1) * rows, :]
            g = blk[i, (heads + h) * rows : (heads + h + 1) * rows, :]
            k = k_ref[:, cols]
            v = v_ref[:, cols]
            mult = mult_ref[h]
            nt = (((1,), (1,)), ((), ()))
            raw = lax.dot_general(q, k, nt, preferred_element_type=F32) * factor
            dprob = lax.dot_general(g, v, nt, preferred_element_type=F32)
            prob = jnp.where(mask, jnp.exp(mult * raw - columns[0:rows, h : h + 1]), 0.0)
            ds = prob * (dprob - columns[0:rows, heads + h : heads + h + 1])
            tau_acc[h] += jnp.sum((ds * raw).reshape(rows // 8, 8, ks), axis=0)
            gb = ((mult * factor) * ds).astype(BF16)
            prob_s[h, at, :] = prob.astype(BF16)
            grad_s[h, at, :] = gb
            term = jnp.dot(gb, k, preferred_element_type=F32)
            if own:
                dq0[h * rows : (h + 1) * rows, :] = term
            else:
                dqs[i, h * rows : (h + 1) * rows, :] = term.astype(BF16)

    tile(0, True)

    @pl.loop(1, n_rows)
    def _(i):
        for which in second:
            exchange_copy(i, which).wait_recv()
        tile(i, False)
        term_copy(i).start()

    tau_a[flat] = jnp.sum(tau_acc[...], axis=1)

    def tau_copy(t):
        peer = lax.rem(flat + t, n_flat)
        return pltpu.make_async_remote_copy(
            src_ref=tau_a.at[flat], dst_ref=tau_a.at[flat],
            send_sem=sta.at[t], recv_sem=rta.at[t],
            device_id={"qrow": lax.rem(peer, n_rows), "dp": peer // n_rows}, device_id_type=MESH,
        )

    def tau_wait(t):
        peer = lax.rem(flat + t, n_flat)
        source = lax.rem(flat - t + n_flat, n_flat)
        pltpu.make_async_remote_copy(
            src_ref=tau_a.at[source], dst_ref=tau_a.at[source],
            send_sem=sta.at[t], recv_sem=rta.at[t],
            device_id={"qrow": lax.rem(peer, n_rows), "dp": peer // n_rows}, device_id_type=MESH,
        ).wait_recv()

    @pl.loop(1, n_flat)
    def _(t):
        tau_copy(t).start()

    tn = (((0,), (0,)), ((), ()))

    def keys(h):
        cols = slice(h * depth, (h + 1) * depth)
        q_all = blk[:, h * rows : (h + 1) * rows, :].reshape(n_rows * rows, depth)
        g_all = blk[:, (heads + h) * rows : (heads + h + 1) * rows, :].reshape(n_rows * rows, depth)
        dk_ref[:, cols] = lax.dot_general(
            grad_s[h], q_all, tn, preferred_element_type=F32
        ).astype(BF16)
        dv_ref[:, cols] = lax.dot_general(
            prob_s[h], g_all, tn, preferred_element_type=F32
        ).astype(BF16)

    for h in range(heads // 2):
        keys(h)

    @pl.loop(1, n_rows)
    def _(i):
        term_copy(i).wait_recv()
        dq0[...] += dqr[i].astype(F32)

    for z in range(n_cols):
        for h in range(heads):
            pack32[h * qs : (h + 1) * qs, :] = dq0[h * rows + z * qs : h * rows + (z + 1) * qs, :]
        dqz[0, z] = pack32[0:hq, :].astype(BF16)

    @pl.loop(1, n_flat)
    def _(t):
        tau_wait(t)

    tau_b[kcol] = jnp.sum(
        tau_a[...].reshape(n_dp, n_rows, heads, 128), axis=1
    ).reshape(n_dp * heads, 128)

    def last_copy(j):
        z = lax.rem(kcol + j, n_cols)
        return pltpu.make_async_remote_copy(
            src_ref=dqz.at[0, z], dst_ref=dqz.at[1, j],
            send_sem=sb.at[j], recv_sem=rb.at[j], device_id={"kcol": z}, device_id_type=MESH,
        )

    def last_tau(j):
        return pltpu.make_async_remote_copy(
            src_ref=tau_b.at[kcol], dst_ref=tau_b.at[kcol],
            send_sem=stb.at[j], recv_sem=rtb.at[j],
            device_id={"kcol": lax.rem(kcol + j, n_cols)}, device_id_type=MESH,
        )

    def last_tau_wait(j):
        source = lax.rem(kcol - j + n_cols, n_cols)
        pltpu.make_async_remote_copy(
            src_ref=tau_b.at[source], dst_ref=tau_b.at[source],
            send_sem=stb.at[j], recv_sem=rtb.at[j],
            device_id={"kcol": lax.rem(kcol + j, n_cols)}, device_id_type=MESH,
        ).wait_recv()

    @pl.loop(1, n_cols)
    def _(j):
        last_copy(j).start()
        last_tau(j).start()

    for h in range(heads // 2, heads):
        keys(h)

    pack32[0:hq, :] = dqz[0, kcol].astype(F32)

    @pl.loop(1, n_cols)
    def _(j):
        last_copy(j).wait_recv()
        pack32[0:hq, :] += dqz[1, j].astype(F32)

    for h in range(heads):
        dq_ref[:, h * depth : (h + 1) * depth] = pack32[h * qs : (h + 1) * qs, :].astype(BF16)

    @pl.loop(1, n_cols)
    def _(j):
        last_tau_wait(j)

    tau = jnp.sum(tau_b[...], axis=0)
    tau = jnp.concatenate([tau, jnp.zeros((128 - n_dp * heads, 128), F32)], axis=0).T
    tau_ref[...] = jnp.sum(tau, axis=0, keepdims=True)[:, 0 : n_dp * heads]

    @pl.loop(1, n_cols)
    def _(j):
        for which in first:
            gather_copy(j, which).wait_send()
        last_copy(j).wait_send()
        last_tau(j).wait_send()

    @pl.loop(1, n_rows)
    def _(i):
        for which in second:
            exchange_copy(i, which).wait_send()
        term_copy(i).wait_send()

    @pl.loop(1, n_flat)
    def _(t):
        tau_copy(t).wait_send()


def local(q, k, v, o, g, lse, mult, spans):
    heads = mult.shape[0]
    qs, width = q.shape
    ks = k.shape[0]
    depth = width // heads
    n_rows = lax.axis_size("qrow")
    n_cols = lax.axis_size("kcol")
    n_dp = lax.axis_size("dp")
    rows = n_cols * qs
    lanes = -(-rows // 128) * 128
    dims = (n_rows, n_cols, n_dp, heads, depth, qs, ks, lanes)
    n_flat = n_rows * n_dp
    vmem = pl.BlockSpec(memory_space=pltpu.VMEM)
    smem = pl.BlockSpec(memory_space=pltpu.SMEM)
    dma = pltpu.SemaphoreType.DMA
    macs = 5 * heads * n_rows * rows * ks * depth
    dq, dk, dv, tau = pl.pallas_call(
        functools.partial(kernel, dims),
        out_shape=(
            jax.ShapeDtypeStruct((qs, width), BF16),
            jax.ShapeDtypeStruct((ks, width), BF16),
            jax.ShapeDtypeStruct((ks, width), BF16),
            jax.ShapeDtypeStruct((1, n_dp * heads), F32),
        ),
        in_specs=[vmem] * 6 + [smem] * 2,
        out_specs=(vmem,) * 4,
        scratch_shapes=[
            pltpu.VMEM((2 * heads * qs, depth), F32),
            pltpu.VMEM((2 * heads * rows, depth), F32),
            pltpu.VMEM((n_cols, 2 * heads * qs, depth), BF16),
            pltpu.VMEM((n_cols, 2 * heads, lanes), F32),
            pltpu.VMEM((n_rows, 2 * heads * rows, depth), BF16),
            pltpu.VMEM((n_rows, 2 * heads, lanes), F32),
            pltpu.VMEM((heads, n_rows * rows, ks), BF16),
            pltpu.VMEM((heads, n_rows * rows, ks), BF16),
            pltpu.VMEM((n_rows, heads * rows, depth), BF16),
            pltpu.VMEM((n_rows, heads * rows, depth), BF16),
            pltpu.VMEM((heads * rows, depth), F32),
            pltpu.VMEM((2, n_cols, heads * qs, depth), BF16),
            pltpu.VMEM((heads, 8, ks), F32),
            pltpu.VMEM((n_flat, heads, 128), F32),
            pltpu.VMEM((n_cols, n_dp * heads, 128), F32),
            dma((n_cols,)), dma((n_cols,)), dma((n_cols,)), dma((n_cols,)),
            dma((n_rows,)), dma((n_rows,)), dma((n_rows,)), dma((n_rows,)),
            dma((n_rows,)), dma((n_rows,)), dma((n_cols,)), dma((n_cols,)),
            dma((n_flat,)), dma((n_flat,)), dma((n_cols,)), dma((n_cols,)),
        ],
        compiler_params=pltpu.CompilerParams(
            collective_id=0, has_side_effects=True, vmem_limit_bytes=56 * 1024 * 1024
        ),
        cost_estimate=pl.CostEstimate(
            flops=2 * macs, bytes_accessed=8 * ks * width, transcendentals=heads * n_rows * rows * ks
        ),
    )(q, k, v, o, g, lse, mult, spans)
    return dq, dk, dv, tau.reshape(-1)


def solution(mesh):
    in_specs = (
        P(("qrow", "kcol"), "dp"),
        P(("kcol", "qrow"), "dp"),
        P(("kcol", "qrow"), "dp"),
        P(("qrow", "kcol"), "dp"),
        P(("qrow", "kcol"), "dp"),
        P("dp", ("qrow", "kcol")),
        P("dp"),
        P(),
    )
    out_specs = (
        P(("qrow", "kcol"), "dp"),
        P(("kcol", "qrow"), "dp"),
        P(("kcol", "qrow"), "dp"),
        P(),
    )
    return jax.shard_map(local, mesh=mesh, in_specs=in_specs, out_specs=out_specs, check_vma=False)
```

```python
import functools
import math

import jax
import jax.numpy as jnp
from jax import lax
from jax.experimental import pallas as pl
from jax.experimental.pallas import tpu as pltpu
from jax.sharding import PartitionSpec as P

MESH = pl.DeviceIdType.MESH
F32 = jnp.float32
BF16 = jnp.bfloat16


CHUNKS = 2


def kernel(
    dims,
    q_ref, k_hbm, v_hbm, o_ref, g_ref, lse_ref, mult_ref, spans_ref,
    dq_ref, dk_hbm, dv_hbm, tau_ref,
    k_ref, v_ref, dk_ref, dv_ref, pack32, asm32, gath, stat1, blk, stat, cols_s, mask_s,
    prob_s, grad_s, dqs, dqr, dq0, dqz, tau_acc, tau_a, tau_b,
    local_sem, s1, r1, s1s, r1s, s2, r2, s2s, r2s, sa, ra, sb, rb, sta, rta, stb, rtb,
):
    n_rows, n_cols, n_dp, heads, depth, qs, ks, lanes, chunks = dims
    hc = heads // chunks
    rows = n_cols * qs
    half = hc * qs
    qrow = lax.axis_index("qrow")
    kcol = lax.axis_index("kcol")
    dp = lax.axis_index("dp")
    flat = dp * n_rows + qrow
    n_flat = n_dp * n_rows
    offset = (ks - qs) * n_rows * n_cols
    factor = 1.0 / math.sqrt(depth)

    barrier = pltpu.get_barrier_semaphore()

    @pl.loop(1, n_cols)
    def _(j):
        pl.semaphore_signal(
            barrier, inc=1, device_id={"kcol": lax.rem(kcol + j, n_cols)}, device_id_type=MESH
        )

    @pl.loop(1, n_flat)
    def _(t):
        peer = lax.rem(flat + t, n_flat)
        pl.semaphore_signal(
            barrier,
            inc=1,
            device_id={"qrow": lax.rem(peer, n_rows), "dp": peer // n_rows},
            device_id_type=MESH,
        )

    load_k = pltpu.make_async_copy(k_hbm, k_ref, local_sem.at[0])
    load_v = pltpu.make_async_copy(v_hbm, v_ref, local_sem.at[1])
    load_k.start()
    load_v.start()

    q32 = q_ref[...].astype(F32)
    g32 = g_ref[...].astype(F32)
    for c in range(chunks):
        for e in range(hc):
            h = c * hc + e
            cols = slice(h * depth, (h + 1) * depth)
            pack32[e * qs : (e + 1) * qs, :] = q32[:, cols]
            pack32[half + e * qs : half + (e + 1) * qs, :] = g32[:, cols]
        gath[c, kcol] = pack32[...].astype(BF16)
    prod = g32 * o_ref[...].astype(F32)
    lane = lax.broadcasted_iota(jnp.int32, (qs, 128), 1)
    delta = jnp.zeros((qs, 128), F32)
    for h in range(heads):
        part = jnp.sum(prod[:, h * depth : (h + 1) * depth], axis=1, keepdims=True)
        delta = jnp.where(lane == h, part, delta)
    asm32[0:128, :] = jnp.zeros((128, 128), F32)
    asm32[0:qs, :] = delta
    delta_t = asm32[0:128, :].T
    asm32[0:heads, :] = jnp.zeros((heads, 128), F32)
    asm32[0:heads, 0:qs] = lse_ref[...]
    both = jnp.concatenate([asm32[0:heads, :], delta_t[0:heads, :]], axis=0)
    if lanes > 128:
        both = jnp.concatenate([both, jnp.zeros((2 * heads, lanes - 128), F32)], axis=1)
    stat1[kcol] = pltpu.roll(both, kcol * qs, 1)
    tau_acc[...] = jnp.zeros_like(tau_acc)

    pl.semaphore_wait(barrier, n_cols - 1 + n_flat - 1)

    def gather_copy(j, c, slot):
        return pltpu.make_async_remote_copy(
            src_ref=gath.at[c, slot], dst_ref=gath.at[c, slot],
            send_sem=s1.at[c, j], recv_sem=r1.at[c, j],
            device_id={"kcol": lax.rem(kcol + j, n_cols)}, device_id_type=MESH,
        )

    def stat_copy(j, slot):
        return pltpu.make_async_remote_copy(
            src_ref=stat1.at[slot], dst_ref=stat1.at[slot],
            send_sem=s1s.at[j], recv_sem=r1s.at[j],
            device_id={"kcol": lax.rem(kcol + j, n_cols)}, device_id_type=MESH,
        )

    @pl.loop(1, n_cols)
    def _(j):
        stat_copy(j, kcol).start()

    for c in range(chunks):

        @pl.loop(1, n_cols)
        def _(j):
            gather_copy(j, c, kcol).start()

    def exchange_copy(i, c):
        return pltpu.make_async_remote_copy(
            src_ref=blk.at[c, 0], dst_ref=blk.at[c, i],
            send_sem=s2.at[c, i], recv_sem=r2.at[c, i],
            device_id={"qrow": lax.rem(qrow + i, n_rows)}, device_id_type=MESH,
        )

    def exchange_stat(i):
        return pltpu.make_async_remote_copy(
            src_ref=stat.at[0], dst_ref=stat.at[i],
            send_sem=s2s.at[i], recv_sem=r2s.at[i],
            device_id={"qrow": lax.rem(qrow + i, n_rows)}, device_id_type=MESH,
        )

    def term_copy(i, c):
        return pltpu.make_async_remote_copy(
            src_ref=dqs.at[c, i], dst_ref=dqr.at[c, i],
            send_sem=sa.at[c, i], recv_sem=ra.at[c, i],
            device_id={"qrow": lax.rem(qrow - i + n_rows, n_rows)}, device_id_type=MESH,
        )

    def last_copy(j, c):
        z = lax.rem(kcol + j, n_cols)
        return pltpu.make_async_remote_copy(
            src_ref=dqz.at[c, 0, z], dst_ref=dqz.at[c, 1, j],
            send_sem=sb.at[c, j], recv_sem=rb.at[c, j], device_id={"kcol": z}, device_id_type=MESH,
        )

    k_pos = (kcol * n_rows + qrow) * ks + lax.broadcasted_iota(jnp.int32, (rows, ks), 1)

    def columns_of(i):
        cols_s[i] = jnp.concatenate(
            [stat[i], jnp.zeros((128 - 2 * heads, lanes), F32)], axis=0
        ).T[0:rows, :]
        group = lax.rem(qrow - i + n_rows, n_rows)
        q_pos = offset + rows * group + lax.broadcasted_iota(jnp.int32, (rows, ks), 0)
        start = jnp.full((rows, ks), offset, jnp.int32)
        begin = offset
        for d in range(spans_ref.shape[0]):
            start = jnp.where(begin <= q_pos, begin, start)
            begin = begin + spans_ref[d]
        mask = (k_pos <= q_pos) & ((k_pos >= start) | (k_pos < offset))
        mask_s[i] = jnp.where(mask, 1.0, 0.0)

    def tile(i, c, own):
        mask = mask_s[i] > 0.5
        at = pl.ds(pl.multiple_of(i * rows, 16), rows)
        for e in range(hc):
            h = c * hc + e
            cols = slice(h * depth, (h + 1) * depth)
            q = blk[c, i, e * rows : (e + 1) * rows, :]
            g = blk[c, i, (hc + e) * rows : (hc + e + 1) * rows, :]
            k = k_ref[:, cols]
            v = v_ref[:, cols]
            mult = mult_ref[h]
            nt = (((1,), (1,)), ((), ()))
            raw = lax.dot_general(q, k, nt, preferred_element_type=F32) * factor
            dprob = lax.dot_general(g, v, nt, preferred_element_type=F32)
            prob = jnp.where(mask, jnp.exp(mult * raw - cols_s[i, :, h : h + 1]), 0.0)
            ds = prob * (dprob - cols_s[i, :, heads + h : heads + h + 1])
            tau_acc[h] += jnp.sum((ds * raw).reshape(rows // 8, 8, ks), axis=0)
            gb = ((mult * factor) * ds).astype(BF16)
            prob_s[h, at, :] = prob.astype(BF16)
            grad_s[h, at, :] = gb
            term = jnp.dot(gb, k, preferred_element_type=F32)
            if own:
                dq0[c, e * rows : (e + 1) * rows, :] = term
            else:
                dqs[c, i, e * rows : (e + 1) * rows, :] = term.astype(BF16)

    for c in range(chunks):

        @pl.loop(1, n_cols)
        def _(j):
            gather_copy(j, c, lax.rem(kcol - j + n_cols, n_cols)).wait_recv()

        for z in range(n_cols):
            pack32[...] = gath[c, z].astype(F32)
            for e in range(2 * hc):
                asm32[e * rows + z * qs : e * rows + (z + 1) * qs, :] = pack32[e * qs : (e + 1) * qs, :]
        blk[c, 0] = asm32[0 : 2 * hc * rows, :].astype(BF16)

        if c == 0:

            @pl.loop(1, n_cols)
            def _(j):
                stat_copy(j, lax.rem(kcol - j + n_cols, n_cols)).wait_recv()

            total = stat1[0]
            for z in range(1, n_cols):
                total = total + stat1[z]
            stat[0] = total

            @pl.loop(1, n_rows)
            def _(i):
                exchange_stat(i).start()

        @pl.loop(1, n_rows)
        def _(i):
            exchange_copy(i, c).start()

        if c == 0:
            load_k.wait()
            load_v.wait()
            columns_of(0)
        tile(0, c, True)

    pad = dqz.shape[3]

    def settle(c):
        @pl.loop(1, n_rows)
        def _(i):
            term_copy(i, c).wait_recv()
            dq0[c] += dqr[c, i].astype(F32)

        for z in range(n_cols):
            for e in range(hc):
                pack32[e * qs : (e + 1) * qs, :] = dq0[
                    c, e * rows + z * qs : e * rows + (z + 1) * qs, :
                ]
            dqz[c, 0, z] = pack32[0:pad, :].astype(BF16)

        @pl.loop(1, n_cols)
        def _(j):
            last_copy(j, c).start()

    for c in range(chunks):

        @pl.loop(1, n_rows)
        def _(i):
            if c == 0:
                exchange_stat(i).wait_recv()
                columns_of(i)
            exchange_copy(i, c).wait_recv()
            tile(i, c, False)
            term_copy(i, c).start()

        if c >= 1:
            settle(c - 1)

    tau_a[flat] = jnp.sum(tau_acc[...], axis=1)

    def tau_copy(t, slot):
        peer = lax.rem(flat + t, n_flat)
        return pltpu.make_async_remote_copy(
            src_ref=tau_a.at[slot], dst_ref=tau_a.at[slot],
            send_sem=sta.at[t], recv_sem=rta.at[t],
            device_id={"qrow": lax.rem(peer, n_rows), "dp": peer // n_rows}, device_id_type=MESH,
        )

    @pl.loop(1, n_flat)
    def _(t):
        tau_copy(t, flat).start()

    tn = (((0,), (0,)), ((), ()))
    for h in range(heads):
        c, e = h // hc, h % hc
        cols = slice(h * depth, (h + 1) * depth)
        q_all = blk[c, :, e * rows : (e + 1) * rows, :].reshape(n_rows * rows, depth)
        g_all = blk[c, :, (hc + e) * rows : (hc + e + 1) * rows, :].reshape(n_rows * rows, depth)
        dk_ref[:, cols] = lax.dot_general(
            grad_s[h], q_all, tn, preferred_element_type=F32
        ).astype(BF16)
        dv_ref[:, cols] = lax.dot_general(
            prob_s[h], g_all, tn, preferred_element_type=F32
        ).astype(BF16)
    store_k = pltpu.make_async_copy(dk_ref, dk_hbm, local_sem.at[2])
    store_v = pltpu.make_async_copy(dv_ref, dv_hbm, local_sem.at[3])
    store_k.start()
    store_v.start()

    settle(chunks - 1)

    @pl.loop(1, n_flat)
    def _(t):
        tau_copy(t, lax.rem(flat - t + n_flat, n_flat)).wait_recv()

    tau_b[kcol] = jnp.sum(
        tau_a[...].reshape(n_dp, n_rows, heads, 128), axis=1
    ).reshape(n_dp * heads, 128)

    def last_tau(j, slot):
        return pltpu.make_async_remote_copy(
            src_ref=tau_b.at[slot], dst_ref=tau_b.at[slot],
            send_sem=stb.at[j], recv_sem=rtb.at[j],
            device_id={"kcol": lax.rem(kcol + j, n_cols)}, device_id_type=MESH,
        )

    @pl.loop(1, n_cols)
    def _(j):
        last_tau(j, kcol).start()

    for c in range(chunks):
        pack32[0:pad, :] = dqz[c, 0, kcol].astype(F32)

        @pl.loop(1, n_cols)
        def _(j):
            last_copy(j, c).wait_recv()
            pack32[0:pad, :] += dqz[c, 1, j].astype(F32)

        for e in range(hc):
            h = c * hc + e
            dq_ref[:, h * depth : (h + 1) * depth] = pack32[e * qs : (e + 1) * qs, :].astype(BF16)

    @pl.loop(1, n_cols)
    def _(j):
        last_tau(j, lax.rem(kcol - j + n_cols, n_cols)).wait_recv()

    tau = jnp.sum(tau_b[...], axis=0)
    tau = jnp.concatenate([tau, jnp.zeros((128 - n_dp * heads, 128), F32)], axis=0).T
    tau_ref[...] = jnp.sum(tau, axis=0, keepdims=True)[:, 0 : n_dp * heads]

    @pl.loop(1, n_cols)
    def _(j):
        stat_copy(j, kcol).wait_send()
        last_tau(j, kcol).wait_send()
        for c in range(chunks):
            gather_copy(j, c, kcol).wait_send()
            last_copy(j, c).wait_send()

    @pl.loop(1, n_rows)
    def _(i):
        exchange_stat(i).wait_send()
        for c in range(chunks):
            exchange_copy(i, c).wait_send()
            term_copy(i, c).wait_send()

    @pl.loop(1, n_flat)
    def _(t):
        tau_copy(t, flat).wait_send()

    store_k.wait()
    store_v.wait()


def hand_on(dq_in, dk_in, dv_in, tau_in, dq_out, dk_out, dv_out, tau_out):
    dq_out[...] = dq_in[...]
    dk_out[...] = dk_in[...]
    dv_out[...] = dv_in[...]
    tau_out[...] = tau_in[...]


def local(q, k, v, o, g, lse, mult, spans):
    heads = mult.shape[0]
    qs, width = q.shape
    ks = k.shape[0]
    depth = width // heads
    n_rows = lax.axis_size("qrow")
    n_cols = lax.axis_size("kcol")
    n_dp = lax.axis_size("dp")
    rows = n_cols * qs
    lanes = -(-rows // 128) * 128
    chunks = CHUNKS
    hc = heads // chunks
    pad = -(-hc * qs // 16) * 16
    dims = (n_rows, n_cols, n_dp, heads, depth, qs, ks, lanes, chunks)
    n_flat = n_rows * n_dp
    vmem = pl.BlockSpec(memory_space=pltpu.VMEM)
    smem = pl.BlockSpec(memory_space=pltpu.SMEM)
    hbm = pl.BlockSpec(memory_space=pl.ANY)
    dma = pltpu.SemaphoreType.DMA
    macs = 5 * heads * n_rows * rows * ks * depth
    shapes = (
        jax.ShapeDtypeStruct((qs, width), BF16),
        jax.ShapeDtypeStruct((ks, width), BF16),
        jax.ShapeDtypeStruct((ks, width), BF16),
        jax.ShapeDtypeStruct((1, n_dp * heads), F32),
    )
    results = pl.pallas_call(
        functools.partial(kernel, dims),
        out_shape=shapes,
        in_specs=[vmem, hbm, hbm, vmem, vmem, vmem, smem, smem],
        out_specs=(vmem, hbm, hbm, vmem),
        scratch_shapes=[
            pltpu.VMEM((ks, width), BF16),
            pltpu.VMEM((ks, width), BF16),
            pltpu.VMEM((ks, width), BF16),
            pltpu.VMEM((ks, width), BF16),
            pltpu.VMEM((2 * hc * qs, depth), F32),
            pltpu.VMEM((max(128, 2 * hc * rows), depth), F32),
            pltpu.VMEM((chunks, n_cols, 2 * hc * qs, depth), BF16),
            pltpu.VMEM((n_cols, 2 * heads, lanes), F32),
            pltpu.VMEM((chunks, n_rows, 2 * hc * rows, depth), BF16),
            pltpu.VMEM((n_rows, 2 * heads, lanes), F32),
            pltpu.VMEM((n_rows, rows, 128), F32),
            pltpu.VMEM((n_rows, rows, ks), F32),
            pltpu.VMEM((heads, n_rows * rows, ks), BF16),
            pltpu.VMEM((heads, n_rows * rows, ks), BF16),
            pltpu.VMEM((chunks, n_rows, hc * rows, depth), BF16),
            pltpu.VMEM((chunks, n_rows, hc * rows, depth), BF16),
            pltpu.VMEM((chunks, hc * rows, depth), F32),
            pltpu.VMEM((chunks, 2, n_cols, pad, depth), BF16),
            pltpu.VMEM((heads, 8, ks), F32),
            pltpu.VMEM((n_flat, heads, 128), F32),
            pltpu.VMEM((n_cols, n_dp * heads, 128), F32),
            dma((4,)),
            dma((chunks, n_cols)), dma((chunks, n_cols)), dma((n_cols,)), dma((n_cols,)),
            dma((chunks, n_rows)), dma((chunks, n_rows)), dma((n_rows,)), dma((n_rows,)),
            dma((chunks, n_rows)), dma((chunks, n_rows)), dma((chunks, n_cols)), dma((chunks, n_cols)),
            dma((n_flat,)), dma((n_flat,)), dma((n_cols,)), dma((n_cols,)),
        ],
        compiler_params=pltpu.CompilerParams(
            collective_id=0, has_side_effects=True, vmem_limit_bytes=58 * 1024 * 1024
        ),
        cost_estimate=pl.CostEstimate(
            flops=2 * macs, bytes_accessed=8 * ks * width, transcendentals=heads * n_rows * rows * ks
        ),
    )(q, k, v, o, g, lse, mult, spans)
    dq, dk, dv, tau = pl.pallas_call(
        hand_on,
        out_shape=shapes,
        in_specs=[vmem] * 4,
        out_specs=(vmem,) * 4,
    )(*results)
    return dq, dk, dv, tau.reshape(-1)


def solution(mesh):
    in_specs = (
        P(("qrow", "kcol"), "dp"),
        P(("kcol", "qrow"), "dp"),
        P(("kcol", "qrow"), "dp"),
        P(("qrow", "kcol"), "dp"),
        P(("qrow", "kcol"), "dp"),
        P("dp", ("qrow", "kcol")),
        P("dp"),
        P(),
    )
    out_specs = (
        P(("qrow", "kcol"), "dp"),
        P(("kcol", "qrow"), "dp"),
        P(("kcol", "qrow"), "dp"),
        P(),
    )
    return jax.shard_map(local, mesh=mesh, in_specs=in_specs, out_specs=out_specs, check_vma=False)
```

```python
import functools
import math

import jax
import jax.numpy as jnp
from jax import lax
from jax.experimental import pallas as pl
from jax.experimental.pallas import tpu as pltpu
from jax.sharding import PartitionSpec as P

MESH = pl.DeviceIdType.MESH
F32 = jnp.float32
BF16 = jnp.bfloat16


CHUNKS = 2


def kernel(
    dims,
    q_ref, k_hbm, v_hbm, o_ref, g_ref, lse_ref, mult_ref, spans_ref,
    dq_ref, dk_hbm, dv_hbm, tau_ref,
    k_ref, v_ref, dk_ref, dv_ref, pack32, asm32, gath, stat1, blk, stat, cols_s, mask_s,
    prob_s, grad_s, dqs, dqr, dq0, dqz, tau_acc, tau_a, tau_b,
    local_sem, s1, r1, s1s, r1s, s2, r2, s2s, r2s, sa, ra, sb, rb, sta, rta, stb, rtb,
):
    n_rows, n_cols, n_dp, heads, depth, qs, ks, lanes, chunks = dims
    hc = heads // chunks
    rows = n_cols * qs
    half = hc * qs
    qrow = lax.axis_index("qrow")
    kcol = lax.axis_index("kcol")
    dp = lax.axis_index("dp")
    flat = dp * n_rows + qrow
    n_flat = n_dp * n_rows
    offset = (ks - qs) * n_rows * n_cols
    factor = 1.0 / math.sqrt(depth)

    barrier = pltpu.get_barrier_semaphore()

    @pl.loop(1, n_cols)
    def _(j):
        pl.semaphore_signal(
            barrier, inc=1, device_id={"kcol": lax.rem(kcol + j, n_cols)}, device_id_type=MESH
        )

    @pl.loop(1, n_flat)
    def _(t):
        peer = lax.rem(flat + t, n_flat)
        pl.semaphore_signal(
            barrier,
            inc=1,
            device_id={"qrow": lax.rem(peer, n_rows), "dp": peer // n_rows},
            device_id_type=MESH,
        )

    load_k = pltpu.make_async_copy(k_hbm, k_ref, local_sem.at[0])
    load_v = pltpu.make_async_copy(v_hbm, v_ref, local_sem.at[1])
    load_k.start()
    load_v.start()

    q32 = q_ref[...].astype(F32)
    g32 = g_ref[...].astype(F32)
    for c in range(chunks):
        for e in range(hc):
            h = c * hc + e
            cols = slice(h * depth, (h + 1) * depth)
            pack32[e * qs : (e + 1) * qs, :] = q32[:, cols]
            pack32[half + e * qs : half + (e + 1) * qs, :] = g32[:, cols]
        gath[c, kcol] = pack32[...].astype(BF16)
    prod = g32 * o_ref[...].astype(F32)
    lane = lax.broadcasted_iota(jnp.int32, (qs, 128), 1)
    delta = jnp.zeros((qs, 128), F32)
    for h in range(heads):
        part = jnp.sum(prod[:, h * depth : (h + 1) * depth], axis=1, keepdims=True)
        delta = jnp.where(lane == h, part, delta)
    asm32[0:128, :] = jnp.zeros((128, 128), F32)
    asm32[0:qs, :] = delta
    delta_t = asm32[0:128, :].T
    asm32[0:heads, :] = jnp.zeros((heads, 128), F32)
    asm32[0:heads, 0:qs] = lse_ref[...]
    both = jnp.concatenate([asm32[0:heads, :], delta_t[0:heads, :]], axis=0)
    if lanes > 128:
        both = jnp.concatenate([both, jnp.zeros((2 * heads, lanes - 128), F32)], axis=1)
    stat1[kcol] = pltpu.roll(both, kcol * qs, 1)
    tau_acc[...] = jnp.zeros_like(tau_acc)

    pl.semaphore_wait(barrier, n_cols - 1 + n_flat - 1)

    def gather_copy(j, c, slot):
        return pltpu.make_async_remote_copy(
            src_ref=gath.at[c, slot], dst_ref=gath.at[c, slot],
            send_sem=s1.at[c, j], recv_sem=r1.at[c, j],
            device_id={"kcol": lax.rem(kcol + j, n_cols)}, device_id_type=MESH,
        )

    def stat_copy(j, slot):
        return pltpu.make_async_remote_copy(
            src_ref=stat1.at[slot], dst_ref=stat1.at[slot],
            send_sem=s1s.at[j], recv_sem=r1s.at[j],
            device_id={"kcol": lax.rem(kcol + j, n_cols)}, device_id_type=MESH,
        )

    for c in range(chunks):

        @pl.loop(1, n_cols)
        def _(j):
            gather_copy(j, c, kcol).start()
            if c == 0:
                stat_copy(j, kcol).start()

    def exchange_copy(i, c):
        return pltpu.make_async_remote_copy(
            src_ref=blk.at[c, 0], dst_ref=blk.at[c, i],
            send_sem=s2.at[c, i], recv_sem=r2.at[c, i],
            device_id={"qrow": lax.rem(qrow + i, n_rows)}, device_id_type=MESH,
        )

    def exchange_stat(i):
        return pltpu.make_async_remote_copy(
            src_ref=stat.at[0], dst_ref=stat.at[i],
            send_sem=s2s.at[i], recv_sem=r2s.at[i],
            device_id={"qrow": lax.rem(qrow + i, n_rows)}, device_id_type=MESH,
        )

    def term_copy(i, c):
        return pltpu.make_async_remote_copy(
            src_ref=dqs.at[c, i], dst_ref=dqr.at[c, i],
            send_sem=sa.at[c, i], recv_sem=ra.at[c, i],
            device_id={"qrow": lax.rem(qrow - i + n_rows, n_rows)}, device_id_type=MESH,
        )

    def last_copy(j, c):
        z = lax.rem(kcol + j, n_cols)
        return pltpu.make_async_remote_copy(
            src_ref=dqz.at[c, 0, z], dst_ref=dqz.at[c, 1, j],
            send_sem=sb.at[c, j], recv_sem=rb.at[c, j], device_id={"kcol": z}, device_id_type=MESH,
        )

    k_pos = (kcol * n_rows + qrow) * ks + lax.broadcasted_iota(jnp.int32, (rows, ks), 1)

    def columns_of(i):
        cols_s[i] = jnp.concatenate(
            [stat[i], jnp.zeros((128 - 2 * heads, lanes), F32)], axis=0
        ).T[0:rows, :]
        group = lax.rem(qrow - i + n_rows, n_rows)
        q_pos = offset + rows * group + lax.broadcasted_iota(jnp.int32, (rows, ks), 0)
        start = jnp.full((rows, ks), offset, jnp.int32)
        begin = offset
        for d in range(spans_ref.shape[0]):
            start = jnp.where(begin <= q_pos, begin, start)
            begin = begin + spans_ref[d]
        mask = (k_pos <= q_pos) & ((k_pos >= start) | (k_pos < offset))
        mask_s[i] = jnp.where(mask, 1.0, 0.0)

    def tile(i, c, own):
        mask = mask_s[i] > 0.5
        at = pl.ds(pl.multiple_of(i * rows, 16), rows)
        for e in range(hc):
            h = c * hc + e
            cols = slice(h * depth, (h + 1) * depth)
            q = blk[c, i, e * rows : (e + 1) * rows, :]
            g = blk[c, i, (hc + e) * rows : (hc + e + 1) * rows, :]
            k = k_ref[:, cols]
            v = v_ref[:, cols]
            mult = mult_ref[h]
            nt = (((1,), (1,)), ((), ()))
            raw = lax.dot_general(q, k, nt, preferred_element_type=F32) * factor
            dprob = lax.dot_general(g, v, nt, preferred_element_type=F32)
            prob = jnp.where(mask, jnp.exp(mult * raw - cols_s[i, :, h : h + 1]), 0.0)
            ds = prob * (dprob - cols_s[i, :, heads + h : heads + h + 1])
            tau_acc[h] += jnp.sum((ds * raw).reshape(rows // 8, 8, ks), axis=0)
            gb = ((mult * factor) * ds).astype(BF16)
            prob_s[h, at, :] = prob.astype(BF16)
            grad_s[h, at, :] = gb
            term = jnp.dot(gb, k, preferred_element_type=F32)
            if own:
                dq0[c, e * rows : (e + 1) * rows, :] = term
            else:
                dqs[c, i, e * rows : (e + 1) * rows, :] = term.astype(BF16)

    for c in range(chunks):

        @pl.loop(1, n_cols)
        def _(j):
            gather_copy(j, c, lax.rem(kcol - j + n_cols, n_cols)).wait_recv()

        for z in range(n_cols):
            pack32[...] = gath[c, z].astype(F32)
            for e in range(2 * hc):
                asm32[e * rows + z * qs : e * rows + (z + 1) * qs, :] = pack32[e * qs : (e + 1) * qs, :]
        blk[c, 0] = asm32[0 : 2 * hc * rows, :].astype(BF16)

        @pl.loop(1, n_rows)
        def _(i):
            exchange_copy(i, c).start()

        if c == 0:

            @pl.loop(1, n_cols)
            def _(j):
                stat_copy(j, lax.rem(kcol - j + n_cols, n_cols)).wait_recv()

            total = stat1[0]
            for z in range(1, n_cols):
                total = total + stat1[z]
            stat[0] = total

            @pl.loop(1, n_rows)
            def _(i):
                exchange_stat(i).start()


    load_k.wait()
    load_v.wait()
    columns_of(0)
    for c in range(chunks):
        tile(0, c, True)
    pad = dqz.shape[3]

    def settle(c):
        @pl.loop(1, n_rows)
        def _(i):
            term_copy(i, c).wait_recv()
            dq0[c] += dqr[c, i].astype(F32)

        for z in range(n_cols):
            for e in range(hc):
                pack32[e * qs : (e + 1) * qs, :] = dq0[
                    c, e * rows + z * qs : e * rows + (z + 1) * qs, :
                ]
            dqz[c, 0, z] = pack32[0:pad, :].astype(BF16)

        @pl.loop(1, n_cols)
        def _(j):
            last_copy(j, c).start()

    for c in range(chunks):

        @pl.loop(1, n_rows)
        def _(i):
            if c == 0:
                exchange_stat(i).wait_recv()
                columns_of(i)
            exchange_copy(i, c).wait_recv()
            tile(i, c, False)
            term_copy(i, c).start()

        if c >= 1:
            settle(c - 1)

    tau_a[flat] = jnp.sum(tau_acc[...], axis=1)

    def tau_copy(t, slot):
        peer = lax.rem(flat + t, n_flat)
        return pltpu.make_async_remote_copy(
            src_ref=tau_a.at[slot], dst_ref=tau_a.at[slot],
            send_sem=sta.at[t], recv_sem=rta.at[t],
            device_id={"qrow": lax.rem(peer, n_rows), "dp": peer // n_rows}, device_id_type=MESH,
        )

    @pl.loop(1, n_flat)
    def _(t):
        tau_copy(t, flat).start()

    tn = (((0,), (0,)), ((), ()))
    for h in range(heads):
        c, e = h // hc, h % hc
        cols = slice(h * depth, (h + 1) * depth)
        q_all = blk[c, :, e * rows : (e + 1) * rows, :].reshape(n_rows * rows, depth)
        g_all = blk[c, :, (hc + e) * rows : (hc + e + 1) * rows, :].reshape(n_rows * rows, depth)
        dk_ref[:, cols] = lax.dot_general(
            grad_s[h], q_all, tn, preferred_element_type=F32
        ).astype(BF16)
        dv_ref[:, cols] = lax.dot_general(
            prob_s[h], g_all, tn, preferred_element_type=F32
        ).astype(BF16)
    store_k = pltpu.make_async_copy(dk_ref, dk_hbm, local_sem.at[2])
    store_v = pltpu.make_async_copy(dv_ref, dv_hbm, local_sem.at[3])
    store_k.start()
    store_v.start()

    settle(chunks - 1)

    @pl.loop(1, n_flat)
    def _(t):
        tau_copy(t, lax.rem(flat - t + n_flat, n_flat)).wait_recv()

    tau_b[kcol] = jnp.sum(
        tau_a[...].reshape(n_dp, n_rows, heads, 128), axis=1
    ).reshape(n_dp * heads, 128)

    def last_tau(j, slot):
        return pltpu.make_async_remote_copy(
            src_ref=tau_b.at[slot], dst_ref=tau_b.at[slot],
            send_sem=stb.at[j], recv_sem=rtb.at[j],
            device_id={"kcol": lax.rem(kcol + j, n_cols)}, device_id_type=MESH,
        )

    @pl.loop(1, n_cols)
    def _(j):
        last_tau(j, kcol).start()

    for c in range(chunks):
        pack32[0:pad, :] = dqz[c, 0, kcol].astype(F32)

        @pl.loop(1, n_cols)
        def _(j):
            last_copy(j, c).wait_recv()
            pack32[0:pad, :] += dqz[c, 1, j].astype(F32)

        for e in range(hc):
            h = c * hc + e
            dq_ref[:, h * depth : (h + 1) * depth] = pack32[e * qs : (e + 1) * qs, :].astype(BF16)

    @pl.loop(1, n_cols)
    def _(j):
        last_tau(j, lax.rem(kcol - j + n_cols, n_cols)).wait_recv()

    tau = jnp.sum(tau_b[...], axis=0)
    tau = jnp.concatenate([tau, jnp.zeros((128 - n_dp * heads, 128), F32)], axis=0).T
    tau_ref[...] = jnp.sum(tau, axis=0, keepdims=True)[:, 0 : n_dp * heads]

    @pl.loop(1, n_cols)
    def _(j):
        stat_copy(j, kcol).wait_send()
        last_tau(j, kcol).wait_send()
        for c in range(chunks):
            gather_copy(j, c, kcol).wait_send()
            last_copy(j, c).wait_send()

    @pl.loop(1, n_rows)
    def _(i):
        exchange_stat(i).wait_send()
        for c in range(chunks):
            exchange_copy(i, c).wait_send()
            term_copy(i, c).wait_send()

    @pl.loop(1, n_flat)
    def _(t):
        tau_copy(t, flat).wait_send()

    store_k.wait()
    store_v.wait()


def hand_on(dq_in, dk_in, dv_in, tau_in, dq_out, dk_out, dv_out, tau_out):
    dq_out[...] = dq_in[...]
    dk_out[...] = dk_in[...]
    dv_out[...] = dv_in[...]
    tau_out[...] = tau_in[...]


def local(q, k, v, o, g, lse, mult, spans):
    heads = mult.shape[0]
    qs, width = q.shape
    ks = k.shape[0]
    depth = width // heads
    n_rows = lax.axis_size("qrow")
    n_cols = lax.axis_size("kcol")
    n_dp = lax.axis_size("dp")
    rows = n_cols * qs
    lanes = -(-rows // 128) * 128
    chunks = CHUNKS
    hc = heads // chunks
    pad = -(-hc * qs // 16) * 16
    dims = (n_rows, n_cols, n_dp, heads, depth, qs, ks, lanes, chunks)
    n_flat = n_rows * n_dp
    vmem = pl.BlockSpec(memory_space=pltpu.VMEM)
    smem = pl.BlockSpec(memory_space=pltpu.SMEM)
    hbm = pl.BlockSpec(memory_space=pl.ANY)
    dma = pltpu.SemaphoreType.DMA
    macs = 5 * heads * n_rows * rows * ks * depth
    shapes = (
        jax.ShapeDtypeStruct((qs, width), BF16),
        jax.ShapeDtypeStruct((ks, width), BF16),
        jax.ShapeDtypeStruct((ks, width), BF16),
        jax.ShapeDtypeStruct((1, n_dp * heads), F32),
    )
    results = pl.pallas_call(
        functools.partial(kernel, dims),
        out_shape=shapes,
        in_specs=[vmem, hbm, hbm, vmem, vmem, vmem, smem, smem],
        out_specs=(vmem, hbm, hbm, vmem),
        scratch_shapes=[
            pltpu.VMEM((ks, width), BF16),
            pltpu.VMEM((ks, width), BF16),
            pltpu.VMEM((ks, width), BF16),
            pltpu.VMEM((ks, width), BF16),
            pltpu.VMEM((2 * hc * qs, depth), F32),
            pltpu.VMEM((max(128, 2 * hc * rows), depth), F32),
            pltpu.VMEM((chunks, n_cols, 2 * hc * qs, depth), BF16),
            pltpu.VMEM((n_cols, 2 * heads, lanes), F32),
            pltpu.VMEM((chunks, n_rows, 2 * hc * rows, depth), BF16),
            pltpu.VMEM((n_rows, 2 * heads, lanes), F32),
            pltpu.VMEM((n_rows, rows, 128), F32),
            pltpu.VMEM((n_rows, rows, ks), F32),
            pltpu.VMEM((heads, n_rows * rows, ks), BF16),
            pltpu.VMEM((heads, n_rows * rows, ks), BF16),
            pltpu.VMEM((chunks, n_rows, hc * rows, depth), BF16),
            pltpu.VMEM((chunks, n_rows, hc * rows, depth), BF16),
            pltpu.VMEM((chunks, hc * rows, depth), F32),
            pltpu.VMEM((chunks, 2, n_cols, pad, depth), BF16),
            pltpu.VMEM((heads, 8, ks), F32),
            pltpu.VMEM((n_flat, heads, 128), F32),
            pltpu.VMEM((n_cols, n_dp * heads, 128), F32),
            dma((4,)),
            dma((chunks, n_cols)), dma((chunks, n_cols)), dma((n_cols,)), dma((n_cols,)),
            dma((chunks, n_rows)), dma((chunks, n_rows)), dma((n_rows,)), dma((n_rows,)),
            dma((chunks, n_rows)), dma((chunks, n_rows)), dma((chunks, n_cols)), dma((chunks, n_cols)),
            dma((n_flat,)), dma((n_flat,)), dma((n_cols,)), dma((n_cols,)),
        ],
        compiler_params=pltpu.CompilerParams(
            collective_id=0, has_side_effects=True, vmem_limit_bytes=58 * 1024 * 1024
        ),
        cost_estimate=pl.CostEstimate(
            flops=2 * macs, bytes_accessed=8 * ks * width, transcendentals=heads * n_rows * rows * ks
        ),
    )(q, k, v, o, g, lse, mult, spans)
    dq, dk, dv, tau = pl.pallas_call(
        hand_on,
        out_shape=shapes,
        grid=(2,),
        in_specs=[
            pl.BlockSpec((qs, width // 2), lambda n: (0, n)),
            pl.BlockSpec((ks // 2, width), lambda n: (n, 0)),
            pl.BlockSpec((ks // 2, width), lambda n: (n, 0)),
            pl.BlockSpec((1, n_dp * heads), lambda n: (0, 0)),
        ],
        out_specs=(
            pl.BlockSpec((qs, width // 2), lambda n: (0, n)),
            pl.BlockSpec((ks // 2, width), lambda n: (n, 0)),
            pl.BlockSpec((ks // 2, width), lambda n: (n, 0)),
            pl.BlockSpec((1, n_dp * heads), lambda n: (0, 0)),
        ),
    )(*results)
    return dq, dk, dv, tau.reshape(-1)


def solution(mesh):
    in_specs = (
        P(("qrow", "kcol"), "dp"),
        P(("kcol", "qrow"), "dp"),
        P(("kcol", "qrow"), "dp"),
        P(("qrow", "kcol"), "dp"),
        P(("qrow", "kcol"), "dp"),
        P("dp", ("qrow", "kcol")),
        P("dp"),
        P(),
    )
    out_specs = (
        P(("qrow", "kcol"), "dp"),
        P(("kcol", "qrow"), "dp"),
        P(("kcol", "qrow"), "dp"),
        P(),
    )
    return jax.shard_map(local, mesh=mesh, in_specs=in_specs, out_specs=out_specs, check_vma=False)
```
